32 devices in a mesh: groups: 2 (over y), wide: 4 (over z), narrow: 4 (over x, core).
Axes of the slice: x: 2, y: 2, z: 4, core: 2. Of those that a mesh axis runs over, the one named last changes fastest.
Arguments:
- projected: bfloat16 [3, 512, 2048], P(None, ('groups', 'wide', 'narrow')), parts along dimension 1, may hold values from -6 to 6
- latents: bfloat16 [512, 2048], P(('groups', 'wide', 'narrow')), parts along dimension 0, may hold values from -6 to 6
- modulation: float32 [8, 2048], P('groups'), parts along dimension 0, may hold values from -3 to 3
- routes: int32 [512, 2], P(('groups', 'wide')), parts along dimension 0, may hold values from 0 to 7, all different within a row; in each aligned block of 64 rows (0 to 63, 64 to 127, ...) at most 24 rows name the same one
- route_weights: float32 [512, 2], P(('groups', 'wide')), parts along dimension 0, may hold values from 0.2 to 1
- out_proj: bfloat16 [2048, 2048], P('narrow'), may hold values from -0.75 to 0.75
- expert_up: bfloat16 [8, 2048, 4096], P('wide', None, 'narrow'), may hold values from -0.125 to 0.125
- expert_down: bfloat16 [8, 4096, 2048], P('wide', 'narrow'), may hold values from -0.09375 to 0.09375
Outputs:
- updated: bfloat16 [512, 2048], P(('groups', 'wide', 'narrow')), parts along dimension 0
The draws below stay inside these ranges and needn't reach their ends.
There are 2 independent parts, one for each index of `groups`. The reference program is written for one: setup_inputs(seed, part) draws one part's arguments, and reference() takes and returns one part's arrays. A program takes and returns all parts, laid end to end along the dimension named above; an argument that names none is the same for every part. Nothing has to cross between parts.
Inputs may be any that keep to these rules, and one draw needn't show every extreme that they name: `routes`: each row names two different experts. In each aligned block of 64 rows no expert is named by more than 24 rows, and in every draw some expert is named by exactly 24 rows of some block.
All inputs are finite; a program needn't handle non-finite values.
Results may differ from the reference program's by a relative error of at most 0.012.
Values may be sent and summed in bfloat16 or wider, within the bound.
A program may use at most 64 MiB of HBM per device.

```python
import math
import jax
import jax.numpy as jnp
import numpy as np
from jax import lax

D = 2048
HEADS = 32
HEAD_DIM = 64
EXPERT_FF = 4096
EXPERTS = 8
SEQ = 256
SHARD_ROWS = 64
MOST = 24
NARROW_BLOCKS = 4
N_WIDE = 4


def draw_projected(key, part):
    key = jax.random.fold_in(key, 11)
    base_key = jax.random.fold_in(key, 0)
    drawn = jnp.clip(1.5 * jax.random.normal(base_key, (3, SEQ, D), jnp.float32), -6.0, 6.0)
    return drawn.astype(jnp.bfloat16)


def level_of(own_key, shape, shards, smallest, high):
    gain, own = 1.0, jax.random.fold_in(own_key, 6)
    for dim, shards_of in shards:
        steps = jnp.exp(jax.random.uniform(jax.random.fold_in(own, dim), (shards_of,), jnp.float32, smallest / len(shards), high / len(shards)))
        gain = gain * jnp.repeat(steps, shape[dim] // shards_of).reshape([-1 if axis == dim else 1 for axis in range(len(shape))])
    return gain


def shared_out(stream_key, own, number, rows, count, top, limit, lean):
    order = jax.random.permutation(stream_key, count)
    packed, common = load_shares(count, rows * top, limit, lean, True), load_shares(count, rows * top, limit, lean, False)
    places = jnp.arange(count)

    def named(sizes, offset_by):
        used = int((sizes > 0).sum())
        fixed = max(1, used // 4)
        shifted = fixed + (places - fixed + offset_by * (used - fixed)) % max(1, count - fixed)
        return jnp.zeros((count,), jnp.int32).at[order[jnp.where(places < fixed, places, shifted)]].set(jnp.asarray(sizes, jnp.int32))

    sizes = jnp.where(number % 4 == 0, named(packed, number // 4), named(common, number - number // 4 - 1))
    mixed = jax.random.permutation(jax.random.fold_in(own, 3), count)
    source_of, receiver = mixed[0:count // 2 * 2:2], mixed[1:count // 2 * 2:2]
    room = jnp.minimum(sizes[source_of] - 1, limit - sizes[receiver]) // 2
    room = jnp.where((source_of == order[0]) | (receiver == order[0]) | (sizes[receiver] == 0), 0, jnp.maximum(room, 0))
    shifted = jax.random.randint(jax.random.fold_in(own, 4), (count // 2,), 0, 1 << 20) % (room + 1)
    sizes = sizes.at[source_of].add(-shifted).at[receiver].add(shifted)
    members = jnp.searchsorted(jnp.cumsum(sizes), jnp.arange(rows * top), side="right").astype(jnp.int32)
    grid = members.reshape(top, rows).T
    grid = grid[jax.random.permutation(jax.random.fold_in(own, 1), rows)]
    offset_by = jax.random.randint(jax.random.fold_in(own, 2), (rows, 1), 0, top)
    return jnp.take_along_axis(grid, (jnp.arange(top)[None, :] + offset_by) % top, axis=1)


def load_shares(number_of, total, bound, lean, full):
    loads = [(1 << 20) // math.isqrt(rank ** lean) + 1 for rank in range(1, number_of + 1)]
    largest = bound if full else min(bound, max(-(-total // number_of), total * loads[0] // sum(loads)))
    least = 1 if total - largest >= number_of - 1 else 0
    holding, rest = [largest] + [least] * (number_of - 1), total - largest - least * (number_of - 1)
    while rest > 0:
        candidates = [i for i in range(1, number_of) if holding[i] < largest] or [i for i in range(1, number_of) if holding[i] < bound]
        whole, left = sum([loads[i] for i in candidates]), rest
        for i in candidates:
            extra = min(bound - holding[i], max(1, left * loads[i] // whole), rest)
            holding[i] = holding[i] + extra
            rest = rest - extra
    return np.array(holding)


def gaussian(stream_key, dims, spread, bound, cuts=(), kind=jnp.bfloat16):
    entries = spread * jax.random.normal(stream_key, dims, jnp.float32)
    if cuts:
        entries = entries * level_of(stream_key, dims, cuts, -0.22, 0.18)
    return jnp.clip(entries, -bound, bound).astype(kind)


def setup_inputs(seed: int = 0, part: int = 0) -> dict:
    seeds = jax.random.split(jax.random.key(seed), 9)
    own_keys = jax.random.split(jax.random.fold_in(seeds[8], part), 9)
    projected = draw_projected(jax.random.fold_in(jax.random.fold_in(seeds[8], part), 71), part)
    latents = gaussian(own_keys[1], (SEQ, D), 1.0, 6.0, ((0, 16),))
    modulation = gaussian(own_keys[2], (4, D), 0.5, 3.0, (), jnp.float32)
    routes_keys = jax.random.split(jax.random.fold_in(own_keys[3], 1), SEQ // SHARD_ROWS)
    routes_turns = jax.random.permutation(jax.random.fold_in(own_keys[3], 3), SEQ // SHARD_ROWS)
    routes = jax.vmap(lambda own, number: shared_out(jax.random.fold_in(own_keys[3], 2), own, number, SHARD_ROWS, EXPERTS, 2, MOST, 2))(routes_keys, routes_turns).reshape((SEQ, 2))
    route_weights = jnp.clip(0.2 + 0.8 * jax.random.uniform(own_keys[4], (SEQ, 2), jnp.float32) ** level_of(own_keys[4], (SEQ, 2), ((0, 4),), -0.2, 0.2), 0.2, 1.0)
    out_proj = gaussian(seeds[5], (D, D), HEAD_DIM ** -0.5, 0.75, ((0, 4),))
    expert_up = gaussian(seeds[6], (EXPERTS, D, EXPERT_FF), D ** -0.5, 0.125, ((0, 4), (2, 4)))
    expert_down = gaussian(seeds[7], (EXPERTS, EXPERT_FF, D), EXPERT_FF ** -0.5, 0.09375, ((0, 4), (1, 4)))
    return {"projected": projected, "latents": latents, "modulation": modulation, "routes": routes, "route_weights": route_weights, "out_proj": out_proj, "expert_up": expert_up, "expert_down": expert_down}


EPSILON = 1e-06

def slot_numbers(route_block):
    flat_routes = route_block.reshape(-1).astype(jnp.int32)
    onehot_table = (flat_routes[:, None] == jnp.arange(EXPERTS, dtype=jnp.int32)[None, :]).astype(jnp.int32)
    earlier = jnp.cumsum(onehot_table, axis=0, dtype=jnp.int32) - onehot_table
    position = lax.optimization_barrier(jnp.sum(earlier * onehot_table, axis=1, dtype=jnp.int32))
    return (flat_routes * MOST + position).astype(jnp.int32)

def one_head(operands):
    query_head, key_head, value_head = operands
    scores = jnp.dot(query_head, key_head.T, preferred_element_type=jnp.float32) * HEAD_DIM ** (-0.5)
    row_max = lax.optimization_barrier(jnp.max(scores, axis=1, keepdims=True))
    weights = jnp.exp(scores - row_max)
    denominator = lax.optimization_barrier(jnp.sum(weights, axis=1, keepdims=True))
    numerator = jnp.dot(weights.astype(jnp.bfloat16), value_head, preferred_element_type=jnp.float32)
    return (numerator / denominator).astype(jnp.bfloat16)

def add_block(total, operands):
    block_in, block_weight = operands
    term = jnp.dot(block_in, block_weight, preferred_element_type=jnp.float32)
    rounded = lax.optimization_barrier(term.astype(jnp.bfloat16))
    return (total + rounded.astype(jnp.float32), None)

def run_expert(operands):
    rows_in, up_matrix, down_matrix = operands
    row_count = rows_in.shape[0]
    block_units = EXPERT_FF // NARROW_BLOCKS
    hidden_units = jax.nn.gelu(jnp.dot(rows_in, up_matrix, preferred_element_type=jnp.float32), approximate=True).astype(jnp.bfloat16)
    hidden_blocks = hidden_units.reshape(row_count, NARROW_BLOCKS, block_units).transpose(1, 0, 2).astype(jnp.float32)
    down_blocks = down_matrix.reshape(NARROW_BLOCKS, block_units, D).astype(jnp.float32)
    partials = jnp.einsum('brf,bfd->brd', hidden_blocks, down_blocks)
    rounded = lax.optimization_barrier(partials.astype(jnp.bfloat16))
    return lax.optimization_barrier(jnp.sum(rounded.astype(jnp.float32), axis=0)).astype(jnp.bfloat16)

def fill_bucket(rows_in, slots):
    token_ids = (jnp.arange(2 * SHARD_ROWS, dtype=jnp.int32) // 2).astype(jnp.int32)
    slot_table = jnp.full((EXPERTS * MOST,), -1, jnp.int32).at[slots].set(token_ids)
    taken_rows = rows_in[jnp.maximum(slot_table, 0)]
    return jnp.where(slot_table[:, None] >= 0, taken_rows, jnp.zeros_like(taken_rows))

def reference(projected, latents, modulation, routes, route_weights, out_proj, expert_up, expert_down):
    per_head = projected.reshape(3, SEQ, HEADS, HEAD_DIM).transpose(0, 2, 1, 3)
    attended = lax.map(one_head, (per_head[0], per_head[1], per_head[2]))
    attended = attended.transpose(1, 0, 2).reshape(SEQ, D)
    block_width = D // NARROW_BLOCKS
    blocks_in = attended.reshape(SEQ, NARROW_BLOCKS, block_width).transpose(1, 0, 2)
    blocks_weight = out_proj.reshape(NARROW_BLOCKS, block_width, D)
    branch, unused = lax.scan(add_block, jnp.zeros((SEQ, D), jnp.float32), (blocks_in, blocks_weight))
    residual = latents.astype(jnp.float32) + modulation[0][None, :] * branch
    mean_value = lax.optimization_barrier(jnp.mean(residual, axis=1, keepdims=True))
    centered = residual - mean_value
    variance = lax.optimization_barrier(jnp.mean(centered * centered, axis=1, keepdims=True))
    normed = centered * lax.rsqrt(variance + EPSILON)
    expert_in = (normed * (1.0 + modulation[2][None, :]) + modulation[1][None, :]).astype(jnp.bfloat16)
    route_shards = routes.reshape(N_WIDE, SHARD_ROWS, 2)
    slot_ids = jax.vmap(slot_numbers)(route_shards)
    input_shards = expert_in.reshape(N_WIDE, SHARD_ROWS, D)
    buckets = jax.vmap(fill_bucket)(input_shards, slot_ids)
    by_expert = buckets.reshape(N_WIDE, EXPERTS, MOST, D).transpose(1, 0, 2, 3).reshape(EXPERTS, N_WIDE * MOST, D)
    expert_rows = lax.map(run_expert, (by_expert, expert_up, expert_down))
    flat_rows = expert_rows.reshape(EXPERTS * N_WIDE * MOST, D)
    expert_index = (slot_ids // MOST).astype(jnp.int32)
    position = (slot_ids % MOST).astype(jnp.int32)
    shard_index = jnp.arange(N_WIDE, dtype=jnp.int32)[:, None]
    flat_index = (expert_index * (N_WIDE * MOST) + shard_index * MOST + position).astype(jnp.int32).reshape(SEQ, 2)
    picked = flat_rows[flat_index].astype(jnp.float32)
    mixture = lax.optimization_barrier(jnp.sum(route_weights[:, :, None] * picked, axis=1))
    return (residual + modulation[3][None, :] * mixture).astype(jnp.bfloat16)
```

```python
import functools
import jax
import jax.numpy as jnp
from jax import lax
from jax.experimental import pallas as pl
from jax.experimental.pallas import tpu as pltpu
from jax.sharding import PartitionSpec as P

HEAD_DIM = 64


EPSILON = 1e-06


def slot_numbers(route_block, expert_count, most_rows):
    flat_routes = route_block.reshape(-1)
    onehot_table = (
        flat_routes[:, None] == jnp.arange(expert_count, dtype=jnp.int32)[None, :]
    ).astype(jnp.int32)
    earlier = jnp.cumsum(onehot_table, axis=0, dtype=jnp.int32) - onehot_table
    position = jnp.sum(earlier * onehot_table, axis=1, dtype=jnp.int32)
    return flat_routes * most_rows + position


def on_device(
    projected, latents, modulation, routes, route_weights, out_proj, expert_up, expert_down
):
    tok_dev = latents.shape[0]
    model_width = latents.shape[1]
    narrow_count = lax.axis_size("narrow")
    wide_count = lax.axis_size("wide")
    narrow_index = lax.axis_index("narrow")
    shard_rows = tok_dev * narrow_count
    local_width = out_proj.shape[0]
    local_heads = local_width // HEAD_DIM
    regrouped = lax.all_to_all(projected, "narrow", split_axis=2, concat_axis=1, tiled=True)
    queries = regrouped[0].reshape(shard_rows, local_heads, HEAD_DIM)
    scale_factor = HEAD_DIM ** (-0.5)
    row_max = jnp.full((shard_rows, local_heads), -1e30, jnp.float32)
    key_rows = lax.all_gather(regrouped[1], "wide", axis=0, tiled=True).reshape(
        -1, local_heads, HEAD_DIM
    )
    value_rows = lax.all_gather(regrouped[2], "wide", axis=0, tiled=True).reshape(
        -1, local_heads, HEAD_DIM
    )
    scores = (
        jnp.einsum("qhd,khd->qhk", queries, key_rows, preferred_element_type=jnp.float32)
        * scale_factor
    )
    new_max = jnp.maximum(row_max, jnp.max(scores, axis=2))
    weights = jnp.exp(scores - new_max[:, :, None])
    new_total = jnp.sum(weights, axis=2)
    new_accum = jnp.einsum(
        "qhk,khd->qhd", weights.astype(jnp.bfloat16), value_rows, preferred_element_type=jnp.float32
    )
    attended = (
        (new_accum / new_total[:, :, None]).astype(jnp.bfloat16).reshape(shard_rows, local_width)
    )
    branch = lax.psum_scatter(
        jnp.dot(attended, out_proj, preferred_element_type=jnp.float32).astype(jnp.bfloat16),
        "narrow",
        scatter_dimension=0,
        tiled=True,
    ).astype(jnp.float32)
    residual = latents.astype(jnp.float32) + modulation[0][None, :] * branch
    mean_value = jnp.mean(residual, axis=1, keepdims=True)
    centered = residual - mean_value
    variance = jnp.mean(centered * centered, axis=1, keepdims=True)
    normed = centered * lax.rsqrt(variance + EPSILON)
    expert_in = (normed * (1.0 + modulation[2][None, :]) + modulation[1][None, :]).astype(
        jnp.bfloat16
    )
    shard_in = lax.all_gather(expert_in, "narrow", axis=0, tiled=True)
    exp_dev = expert_up.shape[0]
    experts_all = exp_dev * wide_count
    most_rows = 3 * tok_dev * narrow_count // experts_all
    column_slots = exp_dev * most_rows
    slot_ids = slot_numbers(routes, experts_all, most_rows)
    token_ids = jnp.arange(2 * shard_rows, dtype=jnp.int32) // 2
    slot_table = jnp.full((experts_all * most_rows,), -1, jnp.int32).at[slot_ids].set(token_ids)
    taken_rows = shard_in[jnp.maximum(slot_table, 0)]
    bucket = jnp.where(slot_table[:, None] >= 0, taken_rows, jnp.zeros_like(taken_rows)).reshape(
        wide_count, column_slots, model_width
    )
    arrived = lax.all_to_all(bucket, "wide", split_axis=0, concat_axis=0, tiled=True)
    sources = arrived.shape[0]
    grouped = arrived.reshape(sources, exp_dev, most_rows, model_width)
    hidden_units = jax.nn.gelu(
        jnp.einsum("sjmd,jdf->sjmf", grouped, expert_up, preferred_element_type=jnp.float32),
        approximate=True,
    ).astype(jnp.bfloat16)
    partial_rows = jnp.einsum(
        "sjmf,jfd->sjmd", hidden_units, expert_down, preferred_element_type=jnp.float32
    )
    summed = lax.psum(
        partial_rows.reshape(sources, column_slots, model_width).astype(jnp.bfloat16), "narrow"
    )
    returned = lax.all_to_all(summed, "wide", split_axis=0, concat_axis=0, tiled=True)
    flat_returned = returned.reshape(experts_all * most_rows, model_width)
    own_slots = lax.dynamic_slice_in_dim(
        slot_ids.reshape(shard_rows, 2), narrow_index * tok_dev, tok_dev, 0
    )
    own_weights = lax.dynamic_slice_in_dim(route_weights, narrow_index * tok_dev, tok_dev, 0)
    picked = flat_returned[own_slots]
    mixture = jnp.sum(own_weights[:, :, None] * picked.astype(jnp.float32), axis=1)
    updated = residual + modulation[3][None, :] * mixture
    return updated.astype(jnp.bfloat16)


def copy_to(source, target, sent, landed, device):
    return pltpu.make_async_remote_copy(
        src_ref=source,
        dst_ref=target,
        send_sem=sent,
        recv_sem=landed,
        device_id=device,
        device_id_type=pl.DeviceIdType.MESH,
    )


def block_kernel(
    wides,
    chunks,
    proj,
    latents,
    modulation,
    table,
    out_proj_hbm,
    up_hbm,
    down_hbm,
    out,
    out_proj,
    up,
    down,
    qkv,
    att,
    att_all,
    part,
    part_all,
    res,
    rows,
    gates,
    hidden,
    mixed,
    core_in,
    pair,
    x_in,
    quad,
    z_in,
    own_sem,
    q_sent,
    q_land,
    t_sent,
    t_land,
    a_sent,
    a_land,
    b_sent,
    b_land,
    z_sent,
    z_land,
    x_sent,
    x_land,
    c_sent,
    c_land,
    d_sent,
    d_land,
    pc_sent,
    pc_land,
    px_sent,
    px_land,
    pz_sent,
    pz_land,
):
    narrows = 4
    everyone = wides * narrows
    tok = latents.shape[0]
    width = latents.shape[1]
    shard = tok * narrows
    cols = width // everyone
    chunk = width // chunks
    units = up.shape[2]
    g = lax.axis_index("groups")
    w = lax.axis_index("wide")
    n = lax.axis_index("narrow")
    me = w * narrows + n
    x = n // 2
    core = n % 2
    over_x = (g, w, (1 - x) * 2 + core)
    over_core = (g, w, x * 2 + 1 - core)
    wide_of = lambda d: lax.rem(w + d, wides)
    f32, bf16 = jnp.float32, jnp.bfloat16

    load_out = pltpu.make_async_copy(out_proj_hbm, out_proj, own_sem.at[0])
    load_up = pltpu.make_async_copy(up_hbm, up, own_sem.at[1])
    load_down = pltpu.make_async_copy(down_hbm, down, own_sem.at[2])

    barrier = pltpu.get_barrier_semaphore()

    def greet(d, carry):
        other = lax.rem(me + d, everyone)
        pl.semaphore_signal(
            barrier,
            inc=1,
            device_id=(g, other // narrows, other % narrows),
            device_id_type=pl.DeviceIdType.MESH,
        )
        return carry

    lax.fori_loop(1, everyone, greet, 0)
    pl.semaphore_wait(barrier, everyone - 1)

    def head_columns(other):
        first = (other % narrows) * (wides * cols) + (other // narrows) * cols
        return pl.ds(pl.multiple_of(first, 128), cols)

    def qkv_copy(other, landing, d):
        return copy_to(
            proj.at[:, :, head_columns(other)],
            qkv.at[:, landing],
            q_sent.at[d],
            q_land.at[landing],
            (g, other // narrows, other % narrows),
        )

    def send_qkv(d, carry):
        qkv_copy(lax.rem(me + d, everyone), me, d).start()
        return carry

    lax.fori_loop(1, everyone, send_qkv, 0)
    own = pltpu.make_async_copy(
        proj.at[:, :, head_columns(me)], qkv.at[:, me], own_sem.at[3]
    )
    own.start()

    def table_rows(of):
        return gates.at[pl.ds(pl.multiple_of(of * shard, shard), shard)]

    def gate_copy(d, of):
        return copy_to(
            table, table_rows(of), t_sent.at[d], t_land.at[of], (g, wide_of(d), n)
        )

    for d in range(1, wides):
        gate_copy(d, w).start()
    gates[pl.ds(pl.multiple_of(w * shard, shard), shard), :] = table[...]
    load_out.start()
    load_up.start()
    load_down.start()

    def wait_qkv(d, carry):
        other = lax.rem(me + d, everyone)
        qkv_copy(other, other, d).wait_recv()
        return carry

    lax.fori_loop(1, everyone, wait_qkv, 0)
    own.wait()

    seq = everyone * tok
    queries = qkv[0].reshape(seq, cols)
    keys = qkv[1].reshape(seq, cols)
    values = qkv[2].reshape(seq, cols)
    head_of = lax.broadcasted_iota(jnp.int32, (1, cols), 1) // HEAD_DIM
    attended = jnp.zeros((seq, cols), f32)
    for h in range(cols // HEAD_DIM):
        mask = jnp.where(head_of == h, 1.0, 0.0).astype(f32)
        scores = lax.dot_general(
            queries * mask.astype(bf16),
            keys,
            (((1,), (1,)), ((), ())),
            preferred_element_type=f32,
        ) * (HEAD_DIM ** (-0.5))
        weights = jnp.exp(scores - jnp.max(scores, axis=1, keepdims=True))
        total = jnp.sum(weights, axis=1, keepdims=True)
        accum = jnp.dot(weights.astype(bf16), values, preferred_element_type=f32)
        attended = attended + (accum / total) * mask
    att[...] = attended.astype(bf16).reshape(wides, shard, cols)

    def att_copy(d, of):
        return copy_to(
            att.at[wide_of(d)], att_all.at[of], a_sent.at[d], a_land.at[of], (g, wide_of(d), n)
        )

    for d in range(1, wides):
        att_copy(d, w).start()
    att_all[w] = att[w]
    load_out.wait()
    for d in range(1, wides):
        att_copy(d, wide_of(wides - d)).wait_recv()

    heads_in = jnp.concatenate([att_all[i] for i in range(wides)], axis=1)
    part[...] = (
        jnp.dot(heads_in, out_proj[...], preferred_element_type=f32)
        .astype(bf16)
        .reshape(narrows, tok, width)
    )

    def part_copy(d, of):
        to = lax.rem(n + d, narrows)
        return copy_to(part.at[to], part_all.at[of], b_sent.at[d], b_land.at[of], (g, w, to))

    for d in (2, 1, 3):
        part_copy(d, n).start()
    branch = part[n].astype(f32)
    for d in (2, 1, 3):
        of = lax.rem(n + narrows - d, narrows)
        part_copy(d, of).wait_recv()
        branch = branch + part_all[of].astype(f32)

    residual = latents[...].astype(f32) + modulation[0:1, :] * branch
    res[...] = residual
    centered = residual - jnp.mean(residual, axis=1, keepdims=True)
    variance = jnp.mean(centered * centered, axis=1, keepdims=True)
    normed = centered * lax.rsqrt(variance + EPSILON)
    rows[me] = (normed * (1.0 + modulation[2:3, :]) + modulation[1:2, :]).astype(bf16)

    def row_of(wide, narrow):
        return rows.at[wide * narrows + narrow]

    def z_copy(d, of):
        return copy_to(row_of(w, n), row_of(of, n), z_sent.at[d], z_land.at[of], (g, wide_of(d), n))

    def x_copy(of, narrow):
        return copy_to(row_of(of, narrow), row_of(of, narrow), x_sent.at[of], x_land.at[of], over_x)

    def c_copy(of, narrow):
        return copy_to(
            row_of(of, narrow), row_of(of, narrow), c_sent.at[of], c_land.at[of], over_core
        )

    def d_copy(of, narrow):
        return copy_to(
            row_of(of, narrow), row_of(of, narrow), d_sent.at[of], d_land.at[of], over_core
        )

    across = (1 - x) * 2 + core
    for d in range(1, wides):
        z_copy(d, w).start()
    x_copy(w, n).start()
    c_copy(w, n).start()
    for d in range(1, wides):
        of = wide_of(wides - d)
        z_copy(d, of).wait_recv()
        x_copy(of, n).start()
        c_copy(of, n).start()
    for d in range(wides):
        of = wide_of(wides - d)
        x_copy(of, across).wait_recv()
        d_copy(of, across).start()
    for d in range(1, wides):
        gate_copy(d, wide_of(wides - d)).wait_recv()
    load_up.wait()
    for d in range(wides):
        of = wide_of(wides - d)
        c_copy(of, x * 2 + 1 - core).wait_recv()
        d_copy(of, (1 - x) * 2 + 1 - core).wait_recv()

    experts = up.shape[0]
    pieces = max(1, units // 512)
    piece = units // pieces
    lanes = lax.broadcasted_iota(jnp.int32, (1, gates.shape[1]), 1)

    def expand(step, carry):
        e = step // pieces
        first = pl.multiple_of((step % pieces) * piece, piece)
        gate = jnp.sum(
            jnp.where(lanes == w * experts + e, gates[...], 0.0), axis=1, keepdims=True
        )
        made = jnp.dot(
            rows[...].reshape(seq, width),
            up[e, :, pl.ds(first, piece)],
            preferred_element_type=f32,
        )
        made = jax.nn.gelu(made, approximate=True) * gate
        hidden[:, pl.ds(pl.multiple_of(step * piece, piece), piece)] = made.astype(bf16)
        return carry

    lax.fori_loop(0, experts * pieces, expand, 0)
    load_down.wait()

    def core_copy(c):
        return copy_to(
            mixed.at[c, :, :, 1 - core], core_in.at[c], pc_sent.at[c], pc_land.at[c], over_core
        )

    def pair_copy(c):
        return copy_to(pair.at[c, :, 1 - x], x_in.at[c], px_sent.at[c], px_land.at[c], over_x)

    def quad_copy(c, d, of):
        return copy_to(
            quad.at[c, wide_of(d)],
            z_in.at[c, of],
            pz_sent.at[c * wides + d],
            pz_land.at[c * wides + of],
            (g, wide_of(d), n),
        )

    def after_core(c):
        core_copy(c).wait_recv()
        total = mixed[c, :, :, core].astype(f32) + core_in[c].astype(f32)
        pair[c] = total.astype(bf16)
        pair_copy(c).start()

    def after_x(c):
        pair_copy(c).wait_recv()
        quad[c] = (pair[c, :, x].astype(f32) + x_in[c].astype(f32)).astype(bf16)
        for d in range(1, wides):
            quad_copy(c, d, w).start()

    def after_z(c):
        total = quad[c, w].astype(f32)
        for d in range(1, wides):
            of = wide_of(wides - d)
            quad_copy(c, d, of).wait_recv()
            total = total + z_in[c, of].astype(f32)
        at = slice(c * chunk, (c + 1) * chunk)
        out[:, at] = (res[:, at] + modulation[3:4, at] * total).astype(bf16)

    for c in range(chunks):
        made = jnp.dot(
            hidden[...], down[:, c * chunk : (c + 1) * chunk], preferred_element_type=f32
        )
        mixed[c] = made.astype(bf16).reshape(wides, 2, 2, tok, chunk)
        core_copy(c).start()
        if c >= 1:
            after_core(c - 1)
        if c >= 2:
            after_x(c - 2)
    after_core(chunks - 1)
    for c in range(max(0, chunks - 2), chunks):
        after_x(c)
    for c in range(chunks):
        after_z(c)

    def sent_qkv(d, carry):
        qkv_copy(lax.rem(me + d, everyone), me, d).wait_send()
        return carry

    lax.fori_loop(1, everyone, sent_qkv, 0)
    for d in range(1, wides):
        gate_copy(d, w).wait_send()
        att_copy(d, w).wait_send()
        z_copy(d, w).wait_send()
    for d in range(1, narrows):
        part_copy(d, n).wait_send()
    for of in range(wides):
        x_copy(of, n).wait_send()
        c_copy(of, n).wait_send()
        d_copy(of, across).wait_send()
    for c in range(chunks):
        core_copy(c).wait_send()
        pair_copy(c).wait_send()
        for d in range(1, wides):
            quad_copy(c, d, w).wait_send()


def fused(
    projected, latents, modulation, routes, route_weights, out_proj, expert_up, expert_down
):
    wides = lax.axis_size("wide")
    narrows = lax.axis_size("narrow")
    tok, width = latents.shape
    shard = tok * narrows
    seq = shard * wides
    cols = width // (wides * narrows)
    experts, unused, units = expert_up.shape
    chunks = 4
    chunk = width // chunks
    f32, bf16 = jnp.float32, jnp.bfloat16
    lanes = jnp.arange(128, dtype=jnp.int32)
    table = jnp.sum(
        jnp.where(routes[:, :, None] == lanes[None, None, :], route_weights[:, :, None], 0.0),
        axis=1,
    )
    down = expert_down.reshape(experts * units, width)
    vmem = pl.BlockSpec(memory_space=pltpu.VMEM)
    anywhere = pl.BlockSpec(memory_space=pl.ANY)
    dma = pltpu.SemaphoreType.DMA
    everyone = wides * narrows
    sizes = [4, everyone, everyone] + [wides] * 4 + [narrows] * 2 + [wides] * 8
    sizes += [chunks] * 4 + [chunks * wides] * 2
    return pl.pallas_call(
        functools.partial(block_kernel, wides, chunks),
        out_shape=jax.ShapeDtypeStruct((tok, width), bf16),
        in_specs=[vmem] * 4 + [anywhere] * 3,
        out_specs=vmem,
        scratch_shapes=[
            pltpu.VMEM(out_proj.shape, bf16),
            pltpu.VMEM(expert_up.shape, bf16),
            pltpu.VMEM(down.shape, bf16),
            pltpu.VMEM((3, everyone, tok, cols), bf16),
            pltpu.VMEM((wides, shard, cols), bf16),
            pltpu.VMEM((wides, shard, cols), bf16),
            pltpu.VMEM((narrows, tok, width), bf16),
            pltpu.VMEM((narrows, tok, width), bf16),
            pltpu.VMEM((tok, width), f32),
            pltpu.VMEM((everyone, tok, width), bf16),
            pltpu.VMEM((seq, 128), f32),
            pltpu.VMEM((seq, experts * units), bf16),
            pltpu.VMEM((chunks, wides, 2, 2, tok, chunk), bf16),
            pltpu.VMEM((chunks, wides, 2, tok, chunk), bf16),
            pltpu.VMEM((chunks, wides, 2, tok, chunk), bf16),
            pltpu.VMEM((chunks, wides, tok, chunk), bf16),
            pltpu.VMEM((chunks, wides, tok, chunk), bf16),
            pltpu.VMEM((chunks, wides, tok, chunk), bf16),
        ]
        + [dma((size,)) for size in sizes],
        compiler_params=pltpu.CompilerParams(
            collective_id=0, has_side_effects=True, vmem_limit_bytes=52 * 1024 * 1024
        ),
    )(projected, latents, modulation, table, out_proj, expert_up, down)


def solution(mesh):
    in_specs = (
        P(None, ("groups", "wide", "narrow"), None),
        P(("groups", "wide", "narrow"), None),
        P("groups", None),
        P(("groups", "wide"), None),
        P(("groups", "wide"), None),
        P("narrow", None),
        P("wide", None, "narrow"),
        P("wide", "narrow", None),
    )
    out_specs = P(("groups", "wide", "narrow"), None)
    small = mesh.shape["narrow"] == 4 and mesh.shape["wide"] == 4
    return jax.shard_map(
        fused if small else on_device,
        mesh=mesh,
        in_specs=in_specs,
        out_specs=out_specs,
        check_vma=False,
    )
```

```python
import functools
import jax
import jax.numpy as jnp
from jax import lax
from jax.experimental import pallas as pl
from jax.experimental.pallas import tpu as pltpu
from jax.sharding import PartitionSpec as P

HEAD_DIM = 64


EPSILON = 1e-06


def slot_numbers(route_block, expert_count, most_rows):
    flat_routes = route_block.reshape(-1)
    onehot_table = (
        flat_routes[:, None] == jnp.arange(expert_count, dtype=jnp.int32)[None, :]
    ).astype(jnp.int32)
    earlier = jnp.cumsum(onehot_table, axis=0, dtype=jnp.int32) - onehot_table
    position = jnp.sum(earlier * onehot_table, axis=1, dtype=jnp.int32)
    return flat_routes * most_rows + position


def on_device(
    projected, latents, modulation, routes, route_weights, out_proj, expert_up, expert_down
):
    tok_dev = latents.shape[0]
    model_width = latents.shape[1]
    narrow_count = lax.axis_size("narrow")
    wide_count = lax.axis_size("wide")
    narrow_index = lax.axis_index("narrow")
    shard_rows = tok_dev * narrow_count
    local_width = out_proj.shape[0]
    local_heads = local_width // HEAD_DIM
    regrouped = lax.all_to_all(projected, "narrow", split_axis=2, concat_axis=1, tiled=True)
    queries = regrouped[0].reshape(shard_rows, local_heads, HEAD_DIM)
    scale_factor = HEAD_DIM ** (-0.5)
    row_max = jnp.full((shard_rows, local_heads), -1e30, jnp.float32)
    key_rows = lax.all_gather(regrouped[1], "wide", axis=0, tiled=True).reshape(
        -1, local_heads, HEAD_DIM
    )
    value_rows = lax.all_gather(regrouped[2], "wide", axis=0, tiled=True).reshape(
        -1, local_heads, HEAD_DIM
    )
    scores = (
        jnp.einsum("qhd,khd->qhk", queries, key_rows, preferred_element_type=jnp.float32)
        * scale_factor
    )
    new_max = jnp.maximum(row_max, jnp.max(scores, axis=2))
    weights = jnp.exp(scores - new_max[:, :, None])
    new_total = jnp.sum(weights, axis=2)
    new_accum = jnp.einsum(
        "qhk,khd->qhd", weights.astype(jnp.bfloat16), value_rows, preferred_element_type=jnp.float32
    )
    attended = (
        (new_accum / new_total[:, :, None]).astype(jnp.bfloat16).reshape(shard_rows, local_width)
    )
    branch = lax.psum_scatter(
        jnp.dot(attended, out_proj, preferred_element_type=jnp.float32).astype(jnp.bfloat16),
        "narrow",
        scatter_dimension=0,
        tiled=True,
    ).astype(jnp.float32)
    residual = latents.astype(jnp.float32) + modulation[0][None, :] * branch
    mean_value = jnp.mean(residual, axis=1, keepdims=True)
    centered = residual - mean_value
    variance = jnp.mean(centered * centered, axis=1, keepdims=True)
    normed = centered * lax.rsqrt(variance + EPSILON)
    expert_in = (normed * (1.0 + modulation[2][None, :]) + modulation[1][None, :]).astype(
        jnp.bfloat16
    )
    shard_in = lax.all_gather(expert_in, "narrow", axis=0, tiled=True)
    exp_dev = expert_up.shape[0]
    experts_all = exp_dev * wide_count
    most_rows = 3 * tok_dev * narrow_count // experts_all
    column_slots = exp_dev * most_rows
    slot_ids = slot_numbers(routes, experts_all, most_rows)
    token_ids = jnp.arange(2 * shard_rows, dtype=jnp.int32) // 2
    slot_table = jnp.full((experts_all * most_rows,), -1, jnp.int32).at[slot_ids].set(token_ids)
    taken_rows = shard_in[jnp.maximum(slot_table, 0)]
    bucket = jnp.where(slot_table[:, None] >= 0, taken_rows, jnp.zeros_like(taken_rows)).reshape(
        wide_count, column_slots, model_width
    )
    arrived = lax.all_to_all(bucket, "wide", split_axis=0, concat_axis=0, tiled=True)
    sources = arrived.shape[0]
    grouped = arrived.reshape(sources, exp_dev, most_rows, model_width)
    hidden_units = jax.nn.gelu(
        jnp.einsum("sjmd,jdf->sjmf", grouped, expert_up, preferred_element_type=jnp.float32),
        approximate=True,
    ).astype(jnp.bfloat16)
    partial_rows = jnp.einsum(
        "sjmf,jfd->sjmd", hidden_units, expert_down, preferred_element_type=jnp.float32
    )
    summed = lax.psum(
        partial_rows.reshape(sources, column_slots, model_width).astype(jnp.bfloat16), "narrow"
    )
    returned = lax.all_to_all(summed, "wide", split_axis=0, concat_axis=0, tiled=True)
    flat_returned = returned.reshape(experts_all * most_rows, model_width)
    own_slots = lax.dynamic_slice_in_dim(
        slot_ids.reshape(shard_rows, 2), narrow_index * tok_dev, tok_dev, 0
    )
    own_weights = lax.dynamic_slice_in_dim(route_weights, narrow_index * tok_dev, tok_dev, 0)
    picked = flat_returned[own_slots]
    mixture = jnp.sum(own_weights[:, :, None] * picked.astype(jnp.float32), axis=1)
    updated = residual + modulation[3][None, :] * mixture
    return updated.astype(jnp.bfloat16)


def copy_to(source, target, sent, landed, device):
    return pltpu.make_async_remote_copy(
        src_ref=source,
        dst_ref=target,
        send_sem=sent,
        recv_sem=landed,
        device_id=device,
        device_id_type=pl.DeviceIdType.MESH,
    )


def block_kernel(
    wides,
    chunks,
    proj_hbm,
    latents_hbm,
    modulation_hbm,
    routes_hbm,
    weights_hbm,
    out_proj_hbm,
    up_hbm,
    down_hbm,
    out,
    routes,
    route_weights,
    table,
    proj,
    latents,
    modulation,
    out_proj,
    up,
    down,
    qkv,
    att,
    att_all,
    part,
    part_all,
    res,
    rows,
    gates,
    gate_rows,
    hidden,
    mixed,
    core_in,
    pair,
    x_in,
    quad,
    z_in,
    own_sem,
    q_sent,
    q_land,
    t_sent,
    t_land,
    a_sent,
    a_land,
    b_sent,
    b_land,
    z_sent,
    z_land,
    x_sent,
    x_land,
    c_sent,
    c_land,
    d_sent,
    d_land,
    pc_sent,
    pc_land,
    px_sent,
    px_land,
    pz_sent,
    pz_land,
):
    narrows = 4
    everyone = wides * narrows
    tok = latents.shape[0]
    width = latents.shape[1]
    shard = tok * narrows
    cols = width // everyone
    chunk = width // chunks
    units = up.shape[2]
    g = lax.axis_index("groups")
    w = lax.axis_index("wide")
    n = lax.axis_index("narrow")
    me = w * narrows + n
    x = n // 2
    core = n % 2
    over_x = (g, w, (1 - x) * 2 + core)
    over_core = (g, w, x * 2 + 1 - core)
    wide_of = lambda d: lax.rem(w + d, wides)
    f32, bf16 = jnp.float32, jnp.bfloat16

    load_proj = pltpu.make_async_copy(proj_hbm, proj, own_sem.at[4])
    load_latents = pltpu.make_async_copy(latents_hbm, latents, own_sem.at[5])
    load_modulation = pltpu.make_async_copy(modulation_hbm, modulation, own_sem.at[6])
    load_proj.start()
    load_latents.start()
    load_modulation.start()
    load_routes = pltpu.make_async_copy(routes_hbm, routes, own_sem.at[7])
    load_weights = pltpu.make_async_copy(weights_hbm, route_weights, own_sem.at[8])
    load_routes.start()
    load_weights.start()
    load_out = pltpu.make_async_copy(out_proj_hbm, out_proj, own_sem.at[0])
    load_up = pltpu.make_async_copy(up_hbm, up, own_sem.at[1])
    load_down = pltpu.make_async_copy(down_hbm, down, own_sem.at[2])

    barrier = pltpu.get_barrier_semaphore()

    def greet(d, carry):
        other = lax.rem(me + d, everyone)
        pl.semaphore_signal(
            barrier,
            inc=1,
            device_id=(g, other // narrows, other % narrows),
            device_id_type=pl.DeviceIdType.MESH,
        )
        return carry

    lax.fori_loop(1, everyone, greet, 0)
    pl.semaphore_wait(barrier, everyone - 1)
    load_proj.wait()

    def head_columns(other):
        first = (other % narrows) * (wides * cols) + (other // narrows) * cols
        return pl.ds(pl.multiple_of(first, 128), cols)

    def qkv_copy(other, landing, d):
        return copy_to(
            proj.at[:, :, head_columns(other)],
            qkv.at[:, landing],
            q_sent.at[d],
            q_land.at[landing],
            (g, other // narrows, other % narrows),
        )

    def send_qkv(d, carry):
        qkv_copy(lax.rem(me + d, everyone), me, d).start()
        return carry

    lax.fori_loop(1, everyone, send_qkv, 0)
    own = pltpu.make_async_copy(
        proj.at[:, :, head_columns(me)], qkv.at[:, me], own_sem.at[3]
    )
    own.start()

    def gate_copy(d, of):
        return copy_to(table, gates.at[of], t_sent.at[d], t_land.at[of], (g, wide_of(d), n))

    load_routes.wait()
    load_weights.wait()
    named = lax.broadcasted_iota(jnp.int32, (table.shape[0], shard), 0)
    table[:, :shard] = jnp.where(named == routes[0:1, :], route_weights[0:1, :], 0.0) + jnp.where(
        named == routes[1:2, :], route_weights[1:2, :], 0.0
    )
    table[:, shard:] = jnp.zeros((table.shape[0], table.shape[1] - shard), f32)

    for d in range(1, wides):
        gate_copy(d, w).start()
    gates[w] = table[...]
    load_out.start()
    load_up.start()
    load_down.start()

    def wait_qkv(d, carry):
        other = lax.rem(me + d, everyone)
        qkv_copy(other, other, d).wait_recv()
        return carry

    lax.fori_loop(1, everyone, wait_qkv, 0)
    own.wait()

    seq = everyone * tok
    queries = qkv[0].reshape(seq, cols)
    keys = qkv[1].reshape(seq, cols)
    values = qkv[2].reshape(seq, cols)
    head_of = lax.broadcasted_iota(jnp.int32, (1, cols), 1) // HEAD_DIM
    attended = jnp.zeros((seq, cols), f32)
    for h in range(cols // HEAD_DIM):
        mask = jnp.where(head_of == h, 1.0, 0.0).astype(f32)
        scores = lax.dot_general(
            queries * mask.astype(bf16),
            keys,
            (((1,), (1,)), ((), ())),
            preferred_element_type=f32,
        ) * (HEAD_DIM ** (-0.5))
        weights = jnp.exp(scores - jnp.max(scores, axis=1, keepdims=True))
        total = jnp.sum(weights, axis=1, keepdims=True)
        accum = jnp.dot(weights.astype(bf16), values, preferred_element_type=f32)
        attended = attended + (accum / total) * mask
    att[...] = attended.astype(bf16).reshape(wides, shard, cols)

    def att_copy(d, of):
        return copy_to(
            att.at[wide_of(d)], att_all.at[of], a_sent.at[d], a_land.at[of], (g, wide_of(d), n)
        )

    for d in range(1, wides):
        att_copy(d, w).start()
    att_all[w] = att[w]
    load_out.wait()
    for d in range(1, wides):
        att_copy(d, wide_of(wides - d)).wait_recv()

    heads_in = jnp.concatenate([att_all[i] for i in range(wides)], axis=1)
    part[...] = (
        jnp.dot(heads_in, out_proj[...], preferred_element_type=f32)
        .astype(bf16)
        .reshape(narrows, tok, width)
    )

    def part_copy(d, of):
        to = lax.rem(n + d, narrows)
        return copy_to(part.at[to], part_all.at[of], b_sent.at[d], b_land.at[of], (g, w, to))

    for d in (2, 1, 3):
        part_copy(d, n).start()
    load_latents.wait()
    load_modulation.wait()
    branch = part[n].astype(f32)
    for d in (2, 1, 3):
        of = lax.rem(n + narrows - d, narrows)
        part_copy(d, of).wait_recv()
        branch = branch + part_all[of].astype(f32)

    residual = latents[...].astype(f32) + modulation[0:1, :] * branch
    res[...] = residual
    centered = residual - jnp.mean(residual, axis=1, keepdims=True)
    variance = jnp.mean(centered * centered, axis=1, keepdims=True)
    normed = centered * lax.rsqrt(variance + EPSILON)
    rows[me] = (normed * (1.0 + modulation[2:3, :]) + modulation[1:2, :]).astype(bf16)

    def row_of(wide, narrow):
        return rows.at[wide * narrows + narrow]

    def z_copy(d, of):
        return copy_to(row_of(w, n), row_of(of, n), z_sent.at[d], z_land.at[of], (g, wide_of(d), n))

    def x_copy(of, narrow):
        return copy_to(row_of(of, narrow), row_of(of, narrow), x_sent.at[of], x_land.at[of], over_x)

    def c_copy(of, narrow):
        return copy_to(
            row_of(of, narrow), row_of(of, narrow), c_sent.at[of], c_land.at[of], over_core
        )

    def d_copy(of, narrow):
        return copy_to(
            row_of(of, narrow), row_of(of, narrow), d_sent.at[of], d_land.at[of], over_core
        )

    across = (1 - x) * 2 + core
    for d in range(1, wides):
        z_copy(d, w).start()
    x_copy(w, n).start()
    c_copy(w, n).start()
    for d in range(1, wides):
        gate_copy(d, wide_of(wides - d)).wait_recv()
    experts = up.shape[0]
    which = lax.broadcasted_iota(jnp.int32, (table.shape[0], 1), 0)
    for e in range(experts):
        for of in range(wides):
            line = jnp.sum(
                jnp.where(which == w * experts + e, gates[of], 0.0), axis=0, keepdims=True
            )
            square = jnp.broadcast_to(line, (line.shape[1], line.shape[1])).T
            gate_rows[e, of * shard : (of + 1) * shard, :] = square[:shard, :]
    for d in range(1, wides):
        of = wide_of(wides - d)
        z_copy(d, of).wait_recv()
        x_copy(of, n).start()
        c_copy(of, n).start()
    def cross(d):
        of = wide_of(wides - d)
        x_copy(of, across).wait_recv()
        d_copy(of, across).start()

    def gathered(d):
        of = wide_of(wides - d)
        c_copy(of, x * 2 + 1 - core).wait_recv()
        d_copy(of, (1 - x) * 2 + 1 - core).wait_recv()

    pieces = max(1, units // 512)
    piece = units // pieces
    steps = experts * pieces

    def expand(shards, step, carry):
        e = step // pieces
        first = pl.multiple_of((step % pieces) * piece, piece)
        taken = [rows[pl.ds(of * narrows, narrows)].reshape(shard, width) for of in shards]
        made = jnp.dot(
            jnp.concatenate(taken, axis=0),
            up[e, :, pl.ds(first, piece)],
            preferred_element_type=f32,
        )
        made = jax.nn.gelu(made, approximate=True)
        columns = pl.ds(pl.multiple_of(step * piece, piece), piece)
        for k, of in enumerate(shards):
            lines = pl.ds(pl.multiple_of(of * shard, shard), shard)
            scaled = made[k * shard : (k + 1) * shard] * gate_rows[e, lines, 0:1]
            hidden[lines, columns] = scaled.astype(bf16)
        return carry

    half = wides // 2
    near = [wide_of(wides - d) for d in range(half)]
    far = [wide_of(wides - d) for d in range(half, wides)]
    for d in range(half):
        cross(d)
    load_up.wait()
    for d in range(half):
        gathered(d)
    lax.fori_loop(0, steps // 2, functools.partial(expand, near), 0)
    cross(half)
    lax.fori_loop(steps // 2, steps, functools.partial(expand, near), 0)
    for d in range(half + 1, wides):
        cross(d)
    for d in range(half, wides):
        gathered(d)
    lax.fori_loop(0, steps, functools.partial(expand, far), 0)
    load_down.wait()

    def core_copy(c):
        return copy_to(
            mixed.at[c, :, :, 1 - core], core_in.at[c], pc_sent.at[c], pc_land.at[c], over_core
        )

    def pair_copy(c):
        return copy_to(pair.at[c, :, 1 - x], x_in.at[c], px_sent.at[c], px_land.at[c], over_x)

    def quad_copy(c, d, of):
        return copy_to(
            quad.at[c, wide_of(d)],
            z_in.at[c, of],
            pz_sent.at[c * wides + d],
            pz_land.at[c * wides + of],
            (g, wide_of(d), n),
        )

    def after_core(c):
        core_copy(c).wait_recv()
        total = mixed[c, :, :, core].astype(f32) + core_in[c].astype(f32)
        pair[c] = total.astype(bf16)
        pair_copy(c).start()

    def after_x(c):
        pair_copy(c).wait_recv()
        quad[c] = (pair[c, :, x].astype(f32) + x_in[c].astype(f32)).astype(bf16)
        for d in range(1, wides):
            quad_copy(c, d, w).start()

    def after_z(c):
        total = quad[c, w].astype(f32)
        for d in range(1, wides):
            of = wide_of(wides - d)
            quad_copy(c, d, of).wait_recv()
            total = total + z_in[c, of].astype(f32)
        at = slice(c * chunk, (c + 1) * chunk)
        out[:, at] = (res[:, at] + modulation[3:4, at] * total).astype(bf16)

    for c in range(chunks):
        made = jnp.dot(
            hidden[...], down[:, c * chunk : (c + 1) * chunk], preferred_element_type=f32
        )
        mixed[c] = made.astype(bf16).reshape(wides, 2, 2, tok, chunk)
        core_copy(c).start()
        if c >= 1:
            after_core(c - 1)
    after_core(chunks - 1)
    for c in range(chunks):
        after_x(c)
    for c in range(chunks):
        after_z(c)

    def sent_qkv(d, carry):
        qkv_copy(lax.rem(me + d, everyone), me, d).wait_send()
        return carry

    lax.fori_loop(1, everyone, sent_qkv, 0)
    for d in range(1, wides):
        gate_copy(d, w).wait_send()
        att_copy(d, w).wait_send()
        z_copy(d, w).wait_send()
    for d in range(1, narrows):
        part_copy(d, n).wait_send()
    for of in range(wides):
        x_copy(of, n).wait_send()
        c_copy(of, n).wait_send()
        d_copy(of, across).wait_send()
    for c in range(chunks):
        core_copy(c).wait_send()
        pair_copy(c).wait_send()
        for d in range(1, wides):
            quad_copy(c, d, w).wait_send()


def fused(
    projected, latents, modulation, routes, route_weights, out_proj, expert_up, expert_down
):
    wides = lax.axis_size("wide")
    narrows = lax.axis_size("narrow")
    tok, width = latents.shape
    shard = tok * narrows
    seq = shard * wides
    cols = width // (wides * narrows)
    experts, unused, units = expert_up.shape
    chunks = 4
    chunk = width // chunks
    f32, bf16 = jnp.float32, jnp.bfloat16
    down = expert_down.reshape(experts * units, width)
    vmem = pl.BlockSpec(memory_space=pltpu.VMEM)
    hbm = pl.BlockSpec(memory_space=pltpu.HBM)
    dma = pltpu.SemaphoreType.DMA
    everyone = wides * narrows
    sizes = [9, everyone, everyone] + [wides] * 4 + [narrows] * 2 + [wides] * 8
    sizes += [chunks] * 4 + [chunks * wides] * 2
    return pl.pallas_call(
        functools.partial(block_kernel, wides, chunks),
        out_shape=jax.ShapeDtypeStruct((tok, width), bf16),
        in_specs=[hbm] * 8,
        out_specs=vmem,
        scratch_shapes=[
            pltpu.VMEM((2, shard), jnp.int32),
            pltpu.VMEM((2, shard), f32),
            pltpu.VMEM((experts * wides, 128), f32),
            pltpu.VMEM(projected.shape, bf16),
            pltpu.VMEM((tok, width), bf16),
            pltpu.VMEM(modulation.shape, f32),
            pltpu.VMEM(out_proj.shape, bf16),
            pltpu.VMEM(expert_up.shape, bf16),
            pltpu.VMEM(down.shape, bf16),
            pltpu.VMEM((3, everyone, tok, cols), bf16),
            pltpu.VMEM((wides, shard, cols), bf16),
            pltpu.VMEM((wides, shard, cols), bf16),
            pltpu.VMEM((narrows, tok, width), bf16),
            pltpu.VMEM((narrows, tok, width), bf16),
            pltpu.VMEM((tok, width), f32),
            pltpu.VMEM((everyone, tok, width), bf16),
            pltpu.VMEM((wides, experts * wides, 128), f32),
            pltpu.VMEM((experts, seq, 128), f32),
            pltpu.VMEM((seq, experts * units), bf16),
            pltpu.VMEM((chunks, wides, 2, 2, tok, chunk), bf16),
            pltpu.VMEM((chunks, wides, 2, tok, chunk), bf16),
            pltpu.VMEM((chunks, wides, 2, tok, chunk), bf16),
            pltpu.VMEM((chunks, wides, tok, chunk), bf16),
            pltpu.VMEM((chunks, wides, tok, chunk), bf16),
            pltpu.VMEM((chunks, wides, tok, chunk), bf16),
        ]
        + [dma((size,)) for size in sizes],
        compiler_params=pltpu.CompilerParams(
            collective_id=0, has_side_effects=True, vmem_limit_bytes=52 * 1024 * 1024
        ),
    )(projected, latents, modulation, routes.T, route_weights.T, out_proj, expert_up, down)


def solution(mesh):
    in_specs = (
        P(None, ("groups", "wide", "narrow"), None),
        P(("groups", "wide", "narrow"), None),
        P("groups", None),
        P(("groups", "wide"), None),
        P(("groups", "wide"), None),
        P("narrow", None),
        P("wide", None, "narrow"),
        P("wide", "narrow", None),
    )
    out_specs = P(("groups", "wide", "narrow"), None)
    small = mesh.shape["narrow"] == 4 and mesh.shape["wide"] == 4
    return jax.shard_map(
        fused if small else on_device,
        mesh=mesh,
        in_specs=in_specs,
        out_specs=out_specs,
        check_vma=False,
    )
```

```python
import functools
import jax
import jax.numpy as jnp
from jax import lax
from jax.experimental import pallas as pl
from jax.experimental.pallas import tpu as pltpu
from jax.sharding import PartitionSpec as P

HEAD_DIM = 64


EPSILON = 1e-06


def slot_numbers(route_block, expert_count, most_rows):
    flat_routes = route_block.reshape(-1)
    onehot_table = (
        flat_routes[:, None] == jnp.arange(expert_count, dtype=jnp.int32)[None, :]
    ).astype(jnp.int32)
    earlier = jnp.cumsum(onehot_table, axis=0, dtype=jnp.int32) - onehot_table
    position = jnp.sum(earlier * onehot_table, axis=1, dtype=jnp.int32)
    return flat_routes * most_rows + position


def on_device(
    projected, latents, modulation, routes, route_weights, out_proj, expert_up, expert_down
):
    tok_dev = latents.shape[0]
    model_width = latents.shape[1]
    narrow_count = lax.axis_size("narrow")
    wide_count = lax.axis_size("wide")
    narrow_index = lax.axis_index("narrow")
    shard_rows = tok_dev * narrow_count
    local_width = out_proj.shape[0]
    local_heads = local_width // HEAD_DIM
    regrouped = lax.all_to_all(projected, "narrow", split_axis=2, concat_axis=1, tiled=True)
    queries = regrouped[0].reshape(shard_rows, local_heads, HEAD_DIM)
    scale_factor = HEAD_DIM ** (-0.5)
    row_max = jnp.full((shard_rows, local_heads), -1e30, jnp.float32)
    key_rows = lax.all_gather(regrouped[1], "wide", axis=0, tiled=True).reshape(
        -1, local_heads, HEAD_DIM
    )
    value_rows = lax.all_gather(regrouped[2], "wide", axis=0, tiled=True).reshape(
        -1, local_heads, HEAD_DIM
    )
    scores = (
        jnp.einsum("qhd,khd->qhk", queries, key_rows, preferred_element_type=jnp.float32)
        * scale_factor
    )
    new_max = jnp.maximum(row_max, jnp.max(scores, axis=2))
    weights = jnp.exp(scores - new_max[:, :, None])
    new_total = jnp.sum(weights, axis=2)
    new_accum = jnp.einsum(
        "qhk,khd->qhd", weights.astype(jnp.bfloat16), value_rows, preferred_element_type=jnp.float32
    )
    attended = (
        (new_accum / new_total[:, :, None]).astype(jnp.bfloat16).reshape(shard_rows, local_width)
    )
    branch = lax.psum_scatter(
        jnp.dot(attended, out_proj, preferred_element_type=jnp.float32).astype(jnp.bfloat16),
        "narrow",
        scatter_dimension=0,
        tiled=True,
    ).astype(jnp.float32)
    residual = latents.astype(jnp.float32) + modulation[0][None, :] * branch
    mean_value = jnp.mean(residual, axis=1, keepdims=True)
    centered = residual - mean_value
    variance = jnp.mean(centered * centered, axis=1, keepdims=True)
    normed = centered * lax.rsqrt(variance + EPSILON)
    expert_in = (normed * (1.0 + modulation[2][None, :]) + modulation[1][None, :]).astype(
        jnp.bfloat16
    )
    shard_in = lax.all_gather(expert_in, "narrow", axis=0, tiled=True)
    exp_dev = expert_up.shape[0]
    experts_all = exp_dev * wide_count
    most_rows = 3 * tok_dev * narrow_count // experts_all
    column_slots = exp_dev * most_rows
    slot_ids = slot_numbers(routes, experts_all, most_rows)
    token_ids = jnp.arange(2 * shard_rows, dtype=jnp.int32) // 2
    slot_table = jnp.full((experts_all * most_rows,), -1, jnp.int32).at[slot_ids].set(token_ids)
    taken_rows = shard_in[jnp.maximum(slot_table, 0)]
    bucket = jnp.where(slot_table[:, None] >= 0, taken_rows, jnp.zeros_like(taken_rows)).reshape(
        wide_count, column_slots, model_width
    )
    arrived = lax.all_to_all(bucket, "wide", split_axis=0, concat_axis=0, tiled=True)
    sources = arrived.shape[0]
    grouped = arrived.reshape(sources, exp_dev, most_rows, model_width)
    hidden_units = jax.nn.gelu(
        jnp.einsum("sjmd,jdf->sjmf", grouped, expert_up, preferred_element_type=jnp.float32),
        approximate=True,
    ).astype(jnp.bfloat16)
    partial_rows = jnp.einsum(
        "sjmf,jfd->sjmd", hidden_units, expert_down, preferred_element_type=jnp.float32
    )
    summed = lax.psum(
        partial_rows.reshape(sources, column_slots, model_width).astype(jnp.bfloat16), "narrow"
    )
    returned = lax.all_to_all(summed, "wide", split_axis=0, concat_axis=0, tiled=True)
    flat_returned = returned.reshape(experts_all * most_rows, model_width)
    own_slots = lax.dynamic_slice_in_dim(
        slot_ids.reshape(shard_rows, 2), narrow_index * tok_dev, tok_dev, 0
    )
    own_weights = lax.dynamic_slice_in_dim(route_weights, narrow_index * tok_dev, tok_dev, 0)
    picked = flat_returned[own_slots]
    mixture = jnp.sum(own_weights[:, :, None] * picked.astype(jnp.float32), axis=1)
    updated = residual + modulation[3][None, :] * mixture
    return updated.astype(jnp.bfloat16)


def copy_to(source, target, sent, landed, device):
    return pltpu.make_async_remote_copy(
        src_ref=source,
        dst_ref=target,
        send_sem=sent,
        recv_sem=landed,
        device_id=device,
        device_id_type=pl.DeviceIdType.MESH,
    )


def block_kernel(
    wides,
    chunks,
    proj_hbm,
    latents_hbm,
    modulation_hbm,
    routes_hbm,
    weights_hbm,
    out_proj_hbm,
    up_hbm,
    down_hbm,
    out,
    routes,
    route_weights,
    table,
    proj,
    latents,
    modulation,
    out_proj,
    up,
    down,
    qkv,
    att,
    att_all,
    part,
    part_all,
    res,
    rows,
    gates,
    gate_rows,
    hidden,
    mixed,
    core_in,
    pair,
    x_in,
    quad,
    z_in,
    own_sem,
    q_sent,
    q_land,
    t_sent,
    t_land,
    a_sent,
    a_land,
    b_sent,
    b_land,
    z_sent,
    z_land,
    x_sent,
    x_land,
    c_sent,
    c_land,
    d_sent,
    d_land,
    pc_sent,
    pc_land,
    px_sent,
    px_land,
    pz_sent,
    pz_land,
):
    narrows = 4
    everyone = wides * narrows
    tok = latents.shape[0]
    width = latents.shape[1]
    shard = tok * narrows
    cols = width // everyone
    chunk = width // chunks
    units = up.shape[2]
    g = lax.axis_index("groups")
    w = lax.axis_index("wide")
    n = lax.axis_index("narrow")
    me = w * narrows + n
    x = n // 2
    core = n % 2
    over_x = (g, w, (1 - x) * 2 + core)
    over_core = (g, w, x * 2 + 1 - core)
    wide_of = lambda d: lax.rem(w + d, wides)
    f32, bf16 = jnp.float32, jnp.bfloat16

    load_proj = pltpu.make_async_copy(proj_hbm, proj, own_sem.at[4])
    load_latents = pltpu.make_async_copy(latents_hbm, latents, own_sem.at[5])
    load_modulation = pltpu.make_async_copy(modulation_hbm, modulation, own_sem.at[6])
    load_proj.start()
    load_latents.start()
    load_modulation.start()
    load_routes = pltpu.make_async_copy(routes_hbm, routes, own_sem.at[7])
    load_weights = pltpu.make_async_copy(weights_hbm, route_weights, own_sem.at[8])
    load_routes.start()
    load_weights.start()
    load_out = pltpu.make_async_copy(out_proj_hbm, out_proj, own_sem.at[0])
    load_up = pltpu.make_async_copy(up_hbm, up, own_sem.at[1])
    load_down = pltpu.make_async_copy(down_hbm, down, own_sem.at[2])

    barrier = pltpu.get_barrier_semaphore()

    def greet(d, carry):
        other = lax.rem(me + d, everyone)
        pl.semaphore_signal(
            barrier,
            inc=1,
            device_id=(g, other // narrows, other % narrows),
            device_id_type=pl.DeviceIdType.MESH,
        )
        return carry

    lax.fori_loop(1, everyone, greet, 0)
    pl.semaphore_wait(barrier, everyone - 1)
    load_proj.wait()

    def head_columns(other):
        first = (other % narrows) * (wides * cols) + (other // narrows) * cols
        return pl.ds(pl.multiple_of(first, 128), cols)

    def qkv_copy(other, landing, d):
        return copy_to(
            proj.at[:, :, head_columns(other)],
            qkv.at[:, landing],
            q_sent.at[d],
            q_land.at[landing],
            (g, other // narrows, other % narrows),
        )

    def send_qkv(d, carry):
        qkv_copy(lax.rem(me + d, everyone), me, d).start()
        return carry

    lax.fori_loop(1, everyone, send_qkv, 0)
    own = pltpu.make_async_copy(
        proj.at[:, :, head_columns(me)], qkv.at[:, me], own_sem.at[3]
    )
    own.start()

    def gate_copy(d, of):
        return copy_to(table, gates.at[of], t_sent.at[d], t_land.at[of], (g, wide_of(d), n))

    load_routes.wait()
    load_weights.wait()
    named = lax.broadcasted_iota(jnp.int32, (table.shape[0], shard), 0)
    table[:, :shard] = jnp.where(named == routes[0:1, :], route_weights[0:1, :], 0.0) + jnp.where(
        named == routes[1:2, :], route_weights[1:2, :], 0.0
    )
    table[:, shard:] = jnp.zeros((table.shape[0], table.shape[1] - shard), f32)

    for d in range(1, wides):
        gate_copy(d, w).start()
    gates[w] = table[...]
    load_out.start()
    load_up.start()
    load_down.start()

    def wait_qkv(d, carry):
        other = lax.rem(me + d, everyone)
        qkv_copy(other, other, d).wait_recv()
        return carry

    lax.fori_loop(1, everyone, wait_qkv, 0)
    own.wait()

    seq = everyone * tok
    queries = qkv[0].reshape(seq, cols)
    keys = qkv[1].reshape(seq, cols)
    values = qkv[2].reshape(seq, cols)
    head_of = lax.broadcasted_iota(jnp.int32, (1, cols), 1) // HEAD_DIM
    attended = jnp.zeros((seq, cols), f32)
    for h in range(cols // HEAD_DIM):
        mask = jnp.where(head_of == h, 1.0, 0.0).astype(f32)
        scores = lax.dot_general(
            queries * mask.astype(bf16),
            keys,
            (((1,), (1,)), ((), ())),
            preferred_element_type=f32,
        ) * (HEAD_DIM ** (-0.5))
        weights = jnp.exp(scores - jnp.max(scores, axis=1, keepdims=True))
        total = jnp.sum(weights, axis=1, keepdims=True)
        accum = jnp.dot(weights.astype(bf16), values, preferred_element_type=f32)
        attended = attended + (accum / total) * mask
    att[...] = attended.astype(bf16).reshape(wides, shard, cols)

    def att_copy(d, of):
        return copy_to(
            att.at[wide_of(d)], att_all.at[of], a_sent.at[d], a_land.at[of], (g, wide_of(d), n)
        )

    for d in range(1, wides):
        att_copy(d, w).start()
    att_all[w] = att[w]
    load_out.wait()
    for d in range(1, wides):
        att_copy(d, wide_of(wides - d)).wait_recv()

    heads_in = jnp.concatenate([att_all[i] for i in range(wides)], axis=1)
    part[...] = (
        jnp.dot(heads_in, out_proj[...], preferred_element_type=f32)
        .astype(bf16)
        .reshape(narrows, tok, width)
    )

    def part_copy(d, of):
        to = lax.rem(n + d, narrows)
        return copy_to(part.at[to], part_all.at[of], b_sent.at[d], b_land.at[of], (g, w, to))

    for d in (2, 1, 3):
        part_copy(d, n).start()
    load_latents.wait()
    load_modulation.wait()
    branch = part[n].astype(f32)
    for d in (2, 1, 3):
        of = lax.rem(n + narrows - d, narrows)
        part_copy(d, of).wait_recv()
        branch = branch + part_all[of].astype(f32)

    residual = latents[...].astype(f32) + modulation[0:1, :] * branch
    res[...] = residual
    centered = residual - jnp.mean(residual, axis=1, keepdims=True)
    variance = jnp.mean(centered * centered, axis=1, keepdims=True)
    normed = centered * lax.rsqrt(variance + EPSILON)
    rows[me] = (normed * (1.0 + modulation[2:3, :]) + modulation[1:2, :]).astype(bf16)

    def row_of(wide, narrow):
        return rows.at[wide * narrows + narrow]

    def z_copy(d, of):
        return copy_to(row_of(w, n), row_of(of, n), z_sent.at[d], z_land.at[of], (g, wide_of(d), n))

    def x_copy(of, narrow):
        return copy_to(row_of(of, narrow), row_of(of, narrow), x_sent.at[of], x_land.at[of], over_x)

    def c_copy(of, narrow):
        return copy_to(
            row_of(of, narrow), row_of(of, narrow), c_sent.at[of], c_land.at[of], over_core
        )

    def d_copy(of, narrow):
        return copy_to(
            row_of(of, narrow), row_of(of, narrow), d_sent.at[of], d_land.at[of], over_core
        )

    across = (1 - x) * 2 + core
    for d in range(1, wides):
        z_copy(d, w).start()
    x_copy(w, n).start()
    c_copy(w, n).start()
    for d in range(1, wides):
        gate_copy(d, wide_of(wides - d)).wait_recv()
    experts = up.shape[0]
    which = lax.broadcasted_iota(jnp.int32, (table.shape[0], 1), 0)
    for e in range(experts):
        for of in range(wides):
            line = jnp.sum(
                jnp.where(which == w * experts + e, gates[of], 0.0), axis=0, keepdims=True
            )
            square = jnp.broadcast_to(line, (line.shape[1], line.shape[1])).T
            gate_rows[e, of * shard : (of + 1) * shard, :] = square[:shard, :]
    for d in range(1, wides):
        of = wide_of(wides - d)
        z_copy(d, of).wait_recv()
        x_copy(of, n).start()
        c_copy(of, n).start()
    def cross(d):
        of = wide_of(wides - d)
        x_copy(of, across).wait_recv()
        d_copy(of, across).start()

    def gathered(d):
        of = wide_of(wides - d)
        c_copy(of, x * 2 + 1 - core).wait_recv()
        d_copy(of, (1 - x) * 2 + 1 - core).wait_recv()

    pieces = max(1, units // 512)
    piece = units // pieces
    steps = experts * pieces

    def expand(shards, step, carry):
        e = step // pieces
        first = pl.multiple_of((step % pieces) * piece, piece)
        taken = [rows[pl.ds(of * narrows, narrows)].reshape(shard, width) for of in shards]
        made = jnp.dot(
            jnp.concatenate(taken, axis=0),
            up[e, :, pl.ds(first, piece)],
            preferred_element_type=f32,
        )
        made = jax.nn.gelu(made, approximate=True)
        columns = pl.ds(pl.multiple_of(step * piece, piece), piece)
        for k, of in enumerate(shards):
            lines = pl.ds(pl.multiple_of(of * shard, shard), shard)
            scaled = made[k * shard : (k + 1) * shard] * gate_rows[e, lines, 0:1]
            hidden[lines, columns] = scaled.astype(bf16)
        return carry

    half = wides // 2
    near = [wide_of(wides - d) for d in range(half)]
    far = [wide_of(wides - d) for d in range(half, wides)]
    for d in range(half):
        cross(d)
    load_up.wait()
    for d in range(half):
        gathered(d)
    lax.fori_loop(0, steps // 2, functools.partial(expand, near), 0)
    cross(half)
    lax.fori_loop(steps // 2, steps, functools.partial(expand, near), 0)
    for d in range(half + 1, wides):
        cross(d)
    for d in range(half, wides):
        gathered(d)
    lax.fori_loop(0, steps, functools.partial(expand, far), 0)
    load_down.wait()

    def core_copy(c):
        return copy_to(
            mixed.at[c, :, :, 1 - core], core_in.at[c], pc_sent.at[c], pc_land.at[c], over_core
        )

    def pair_copy(c):
        return copy_to(pair.at[c, :, 1 - x], x_in.at[c], px_sent.at[c], px_land.at[c], over_x)

    def quad_copy(c, d, of):
        return copy_to(
            quad.at[c, wide_of(d)],
            z_in.at[c, of],
            pz_sent.at[c * wides + d],
            pz_land.at[c * wides + of],
            (g, wide_of(d), n),
        )

    def after_core(c):
        core_copy(c).wait_recv()
        total = mixed[c, :, :, core].astype(f32) + core_in[c].astype(f32)
        pair[c] = total.astype(bf16)
        pair_copy(c).start()

    def after_x(c):
        pair_copy(c).wait_recv()
        quad[c] = (pair[c, :, x].astype(f32) + x_in[c].astype(f32)).astype(bf16)
        for d in range(1, wides):
            quad_copy(c, d, w).start()

    def after_z(c):
        total = quad[c, w].astype(f32)
        for d in range(1, wides):
            of = wide_of(wides - d)
            quad_copy(c, d, of).wait_recv()
            total = total + z_in[c, of].astype(f32)
        at = slice(c * chunk, (c + 1) * chunk)
        out[:, at] = (res[:, at] + modulation[3:4, at] * total).astype(bf16)

    for c in range(chunks):
        made = jnp.dot(
            hidden[...], down[:, c * chunk : (c + 1) * chunk], preferred_element_type=f32
        )
        mixed[c] = made.astype(bf16).reshape(wides, 2, 2, tok, chunk)
        core_copy(c).start()
        if c >= 1:
            after_core(c - 1)
    after_core(chunks - 1)
    for c in range(chunks):
        after_x(c)
    for c in range(chunks):
        after_z(c)

    def sent_qkv(d, carry):
        qkv_copy(lax.rem(me + d, everyone), me, d).wait_send()
        return carry

    lax.fori_loop(1, everyone, sent_qkv, 0)
    for d in range(1, wides):
        gate_copy(d, w).wait_send()
        att_copy(d, w).wait_send()
        z_copy(d, w).wait_send()
    for d in range(1, narrows):
        part_copy(d, n).wait_send()
    for of in range(wides):
        x_copy(of, n).wait_send()
        c_copy(of, n).wait_send()
        d_copy(of, across).wait_send()
    for c in range(chunks):
        core_copy(c).wait_send()
        pair_copy(c).wait_send()
        for d in range(1, wides):
            quad_copy(c, d, w).wait_send()


def fused(
    projected, latents, modulation, routes, route_weights, out_proj, expert_up, expert_down
):
    wides = lax.axis_size("wide")
    narrows = lax.axis_size("narrow")
    tok, width = latents.shape
    shard = tok * narrows
    seq = shard * wides
    cols = width // (wides * narrows)
    experts, unused, units = expert_up.shape
    chunks = 4
    chunk = width // chunks
    f32, bf16 = jnp.float32, jnp.bfloat16
    down = expert_down.reshape(experts * units, width)
    vmem = pl.BlockSpec(memory_space=pltpu.VMEM)
    hbm = pl.BlockSpec(memory_space=pltpu.HBM)
    dma = pltpu.SemaphoreType.DMA
    everyone = wides * narrows
    sizes = [9, everyone, everyone] + [wides] * 4 + [narrows] * 2 + [wides] * 8
    sizes += [chunks] * 4 + [chunks * wides] * 2
    return pl.pallas_call(
        functools.partial(block_kernel, wides, chunks),
        out_shape=jax.ShapeDtypeStruct((tok, width), bf16),
        in_specs=[hbm] * 8,
        out_specs=vmem,
        scratch_shapes=[
            pltpu.VMEM((2, shard), jnp.int32),
            pltpu.VMEM((2, shard), f32),
            pltpu.VMEM((experts * wides, 128), f32),
            pltpu.VMEM(projected.shape, bf16),
            pltpu.VMEM((tok, width), bf16),
            pltpu.VMEM(modulation.shape, f32),
            pltpu.VMEM(out_proj.shape, bf16),
            pltpu.VMEM(expert_up.shape, bf16),
            pltpu.VMEM(down.shape, bf16),
            pltpu.VMEM((3, everyone, tok, cols), bf16),
            pltpu.VMEM((wides, shard, cols), bf16),
            pltpu.VMEM((wides, shard, cols), bf16),
            pltpu.VMEM((narrows, tok, width), bf16),
            pltpu.VMEM((narrows, tok, width), bf16),
            pltpu.VMEM((tok, width), f32),
            pltpu.VMEM((everyone, tok, width), bf16),
            pltpu.VMEM((wides, experts * wides, 128), f32),
            pltpu.VMEM((experts, seq, 128), f32),
            pltpu.VMEM((seq, experts * units), bf16),
            pltpu.VMEM((chunks, wides, 2, 2, tok, chunk), bf16),
            pltpu.VMEM((chunks, wides, 2, tok, chunk), bf16),
            pltpu.VMEM((chunks, wides, 2, tok, chunk), bf16),
            pltpu.VMEM((chunks, wides, tok, chunk), bf16),
            pltpu.VMEM((chunks, wides, tok, chunk), bf16),
            pltpu.VMEM((chunks, wides, tok, chunk), bf16),
        ]
        + [dma((size,)) for size in sizes],
        compiler_params=pltpu.CompilerParams(
            collective_id=0, has_side_effects=True, vmem_limit_bytes=65400 * 1024
        ),
    )(projected, latents, modulation, routes.T, route_weights.T, out_proj, expert_up, down)


def solution(mesh):
    in_specs = (
        P(None, ("groups", "wide", "narrow"), None),
        P(("groups", "wide", "narrow"), None),
        P("groups", None),
        P(("groups", "wide"), None),
        P(("groups", "wide"), None),
        P("narrow", None),
        P("wide", None, "narrow"),
        P("wide", "narrow", None),
    )
    out_specs = P(("groups", "wide", "narrow"), None)
    small = mesh.shape["narrow"] == 4 and mesh.shape["wide"] == 4
    return jax.shard_map(
        fused if small else on_device,
        mesh=mesh,
        in_specs=in_specs,
        out_specs=out_specs,
        check_vma=False,
    )
```

```python
import functools
import jax
import jax.numpy as jnp
from jax import lax
from jax.experimental import pallas as pl
from jax.experimental.pallas import tpu as pltpu
from jax.sharding import PartitionSpec as P

HEAD_DIM = 64


EPSILON = 1e-06


def slot_numbers(route_block, expert_count, most_rows):
    flat_routes = route_block.reshape(-1)
    onehot_table = (
        flat_routes[:, None] == jnp.arange(expert_count, dtype=jnp.int32)[None, :]
    ).astype(jnp.int32)
    earlier = jnp.cumsum(onehot_table, axis=0, dtype=jnp.int32) - onehot_table
    position = jnp.sum(earlier * onehot_table, axis=1, dtype=jnp.int32)
    return flat_routes * most_rows + position


def on_device(
    projected, latents, modulation, routes, route_weights, out_proj, expert_up, expert_down
):
    tok_dev = latents.shape[0]
    model_width = latents.shape[1]
    narrow_count = lax.axis_size("narrow")
    wide_count = lax.axis_size("wide")
    narrow_index = lax.axis_index("narrow")
    shard_rows = tok_dev * narrow_count
    local_width = out_proj.shape[0]
    local_heads = local_width // HEAD_DIM
    regrouped = lax.all_to_all(projected, "narrow", split_axis=2, concat_axis=1, tiled=True)
    queries = regrouped[0].reshape(shard_rows, local_heads, HEAD_DIM)
    scale_factor = HEAD_DIM ** (-0.5)
    row_max = jnp.full((shard_rows, local_heads), -1e30, jnp.float32)
    key_rows = lax.all_gather(regrouped[1], "wide", axis=0, tiled=True).reshape(
        -1, local_heads, HEAD_DIM
    )
    value_rows = lax.all_gather(regrouped[2], "wide", axis=0, tiled=True).reshape(
        -1, local_heads, HEAD_DIM
    )
    scores = (
        jnp.einsum("qhd,khd->qhk", queries, key_rows, preferred_element_type=jnp.float32)
        * scale_factor
    )
    new_max = jnp.maximum(row_max, jnp.max(scores, axis=2))
    weights = jnp.exp(scores - new_max[:, :, None])
    new_total = jnp.sum(weights, axis=2)
    new_accum = jnp.einsum(
        "qhk,khd->qhd", weights.astype(jnp.bfloat16), value_rows, preferred_element_type=jnp.float32
    )
    attended = (
        (new_accum / new_total[:, :, None]).astype(jnp.bfloat16).reshape(shard_rows, local_width)
    )
    branch = lax.psum_scatter(
        jnp.dot(attended, out_proj, preferred_element_type=jnp.float32).astype(jnp.bfloat16),
        "narrow",
        scatter_dimension=0,
        tiled=True,
    ).astype(jnp.float32)
    residual = latents.astype(jnp.float32) + modulation[0][None, :] * branch
    mean_value = jnp.mean(residual, axis=1, keepdims=True)
    centered = residual - mean_value
    variance = jnp.mean(centered * centered, axis=1, keepdims=True)
    normed = centered * lax.rsqrt(variance + EPSILON)
    expert_in = (normed * (1.0 + modulation[2][None, :]) + modulation[1][None, :]).astype(
        jnp.bfloat16
    )
    shard_in = lax.all_gather(expert_in, "narrow", axis=0, tiled=True)
    exp_dev = expert_up.shape[0]
    experts_all = exp_dev * wide_count
    most_rows = 3 * tok_dev * narrow_count // experts_all
    column_slots = exp_dev * most_rows
    slot_ids = slot_numbers(routes, experts_all, most_rows)
    token_ids = jnp.arange(2 * shard_rows, dtype=jnp.int32) // 2
    slot_table = jnp.full((experts_all * most_rows,), -1, jnp.int32).at[slot_ids].set(token_ids)
    taken_rows = shard_in[jnp.maximum(slot_table, 0)]
    bucket = jnp.where(slot_table[:, None] >= 0, taken_rows, jnp.zeros_like(taken_rows)).reshape(
        wide_count, column_slots, model_width
    )
    arrived = lax.all_to_all(bucket, "wide", split_axis=0, concat_axis=0, tiled=True)
    sources = arrived.shape[0]
    grouped = arrived.reshape(sources, exp_dev, most_rows, model_width)
    hidden_units = jax.nn.gelu(
        jnp.einsum("sjmd,jdf->sjmf", grouped, expert_up, preferred_element_type=jnp.float32),
        approximate=True,
    ).astype(jnp.bfloat16)
    partial_rows = jnp.einsum(
        "sjmf,jfd->sjmd", hidden_units, expert_down, preferred_element_type=jnp.float32
    )
    summed = lax.psum(
        partial_rows.reshape(sources, column_slots, model_width).astype(jnp.bfloat16), "narrow"
    )
    returned = lax.all_to_all(summed, "wide", split_axis=0, concat_axis=0, tiled=True)
    flat_returned = returned.reshape(experts_all * most_rows, model_width)
    own_slots = lax.dynamic_slice_in_dim(
        slot_ids.reshape(shard_rows, 2), narrow_index * tok_dev, tok_dev, 0
    )
    own_weights = lax.dynamic_slice_in_dim(route_weights, narrow_index * tok_dev, tok_dev, 0)
    picked = flat_returned[own_slots]
    mixture = jnp.sum(own_weights[:, :, None] * picked.astype(jnp.float32), axis=1)
    updated = residual + modulation[3][None, :] * mixture
    return updated.astype(jnp.bfloat16)


def copy_to(source, target, sent, landed, device):
    return pltpu.make_async_remote_copy(
        src_ref=source,
        dst_ref=target,
        send_sem=sent,
        recv_sem=landed,
        device_id=device,
        device_id_type=pl.DeviceIdType.MESH,
    )


def block_kernel(
    wides,
    chunks,
    proj_hbm,
    latents_hbm,
    modulation_hbm,
    routes_hbm,
    weights_hbm,
    out_proj_hbm,
    up_hbm,
    down_hbm,
    out,
    routes,
    route_weights,
    table,
    proj,
    latents,
    modulation,
    out_proj,
    up,
    down,
    qkv,
    att,
    att_all,
    part,
    part_all,
    res,
    rows,
    gates,
    gate_rows,
    hidden,
    mixed,
    core_in,
    pair,
    x_in,
    quad,
    z_in,
    own_sem,
    q_sent,
    q_land,
    t_sent,
    t_land,
    a_sent,
    a_land,
    b_sent,
    b_land,
    z_sent,
    z_land,
    x_sent,
    x_land,
    c_sent,
    c_land,
    d_sent,
    d_land,
    pc_sent,
    pc_land,
    px_sent,
    px_land,
    pz_sent,
    pz_land,
):
    narrows = 4
    everyone = wides * narrows
    tok = latents.shape[0]
    width = latents.shape[1]
    shard = tok * narrows
    cols = width // everyone
    chunk = width // chunks
    units = up.shape[2]
    g = lax.axis_index("groups")
    w = lax.axis_index("wide")
    n = lax.axis_index("narrow")
    me = w * narrows + n
    x = n // 2
    core = n % 2
    over_x = (g, w, (1 - x) * 2 + core)
    over_core = (g, w, x * 2 + 1 - core)
    wide_of = lambda d: lax.rem(w + d, wides)
    f32, bf16 = jnp.float32, jnp.bfloat16

    load_proj = pltpu.make_async_copy(proj_hbm, proj, own_sem.at[4])
    load_latents = pltpu.make_async_copy(latents_hbm, latents, own_sem.at[5])
    load_modulation = pltpu.make_async_copy(modulation_hbm, modulation, own_sem.at[6])
    load_proj.start()
    load_latents.start()
    load_modulation.start()
    load_routes = pltpu.make_async_copy(routes_hbm, routes, own_sem.at[7])
    load_weights = pltpu.make_async_copy(weights_hbm, route_weights, own_sem.at[8])
    load_routes.start()
    load_weights.start()
    load_out = pltpu.make_async_copy(out_proj_hbm, out_proj, own_sem.at[0])
    load_up = pltpu.make_async_copy(up_hbm, up, own_sem.at[1])
    load_down = pltpu.make_async_copy(down_hbm, down, own_sem.at[2])
    load_out.start()
    load_up.start()
    load_down.start()

    barrier = pltpu.get_barrier_semaphore()

    def greet(d, carry):
        other = lax.rem(me + d, everyone)
        pl.semaphore_signal(
            barrier,
            inc=1,
            device_id=(g, other // narrows, other % narrows),
            device_id_type=pl.DeviceIdType.MESH,
        )
        return carry

    lax.fori_loop(1, everyone, greet, 0)
    pl.semaphore_wait(barrier, everyone - 1)
    load_proj.wait()

    def head_columns(other):
        first = (other % narrows) * (wides * cols) + (other // narrows) * cols
        return pl.ds(pl.multiple_of(first, 128), cols)

    def qkv_copy(other, landing, d):
        return copy_to(
            proj.at[:, :, head_columns(other)],
            qkv.at[:, landing],
            q_sent.at[d],
            q_land.at[landing],
            (g, other // narrows, other % narrows),
        )

    def send_qkv(d, carry):
        qkv_copy(lax.rem(me + d, everyone), me, d).start()
        return carry

    lax.fori_loop(1, everyone, send_qkv, 0)
    own = pltpu.make_async_copy(
        proj.at[:, :, head_columns(me)], qkv.at[:, me], own_sem.at[3]
    )
    own.start()

    def gate_copy(d, of):
        return copy_to(table, gates.at[of], t_sent.at[d], t_land.at[of], (g, wide_of(d), n))

    load_routes.wait()
    load_weights.wait()
    named = lax.broadcasted_iota(jnp.int32, (table.shape[0], shard), 0)
    table[:, :shard] = jnp.where(named == routes[0:1, :], route_weights[0:1, :], 0.0) + jnp.where(
        named == routes[1:2, :], route_weights[1:2, :], 0.0
    )
    table[:, shard:] = jnp.zeros((table.shape[0], table.shape[1] - shard), f32)

    for d in range(1, wides):
        gate_copy(d, w).start()
    gates[w] = table[...]

    def wait_qkv(d, carry):
        other = lax.rem(me + d, everyone)
        qkv_copy(other, other, d).wait_recv()
        return carry

    lax.fori_loop(1, everyone, wait_qkv, 0)
    own.wait()

    seq = everyone * tok
    queries = qkv[0].reshape(seq, cols)
    keys = qkv[1].reshape(seq, cols)
    values = qkv[2].reshape(seq, cols)
    head_of = lax.broadcasted_iota(jnp.int32, (1, cols), 1) // HEAD_DIM
    attended = jnp.zeros((seq, cols), f32)
    for h in range(cols // HEAD_DIM):
        mask = jnp.where(head_of == h, 1.0, 0.0).astype(f32)
        scores = lax.dot_general(
            queries * mask.astype(bf16),
            keys,
            (((1,), (1,)), ((), ())),
            preferred_element_type=f32,
        ) * (HEAD_DIM ** (-0.5))
        weights = jnp.exp(scores - jnp.max(scores, axis=1, keepdims=True))
        total = jnp.sum(weights, axis=1, keepdims=True)
        accum = jnp.dot(weights.astype(bf16), values, preferred_element_type=f32)
        attended = attended + (accum / total) * mask
    att[...] = attended.astype(bf16).reshape(wides, shard, cols)

    def att_copy(d, of):
        return copy_to(
            att.at[wide_of(d)], att_all.at[of], a_sent.at[d], a_land.at[of], (g, wide_of(d), n)
        )

    for d in range(1, wides):
        att_copy(d, w).start()
    att_all[w] = att[w]
    load_out.wait()
    for d in range(1, wides):
        att_copy(d, wide_of(wides - d)).wait_recv()

    heads_in = jnp.concatenate([att_all[i] for i in range(wides)], axis=1)
    part[...] = (
        jnp.dot(heads_in, out_proj[...], preferred_element_type=f32)
        .astype(bf16)
        .reshape(narrows, tok, width)
    )

    def part_copy(d, of):
        to = lax.rem(n + d, narrows)
        return copy_to(part.at[to], part_all.at[of], b_sent.at[d], b_land.at[of], (g, w, to))

    for d in (2, 1, 3):
        part_copy(d, n).start()
    load_latents.wait()
    load_modulation.wait()
    branch = part[n].astype(f32)
    for d in (2, 1, 3):
        of = lax.rem(n + narrows - d, narrows)
        part_copy(d, of).wait_recv()
        branch = branch + part_all[of].astype(f32)

    residual = latents[...].astype(f32) + modulation[0:1, :] * branch
    res[...] = residual
    centered = residual - jnp.mean(residual, axis=1, keepdims=True)
    variance = jnp.mean(centered * centered, axis=1, keepdims=True)
    normed = centered * lax.rsqrt(variance + EPSILON)
    rows[me] = (normed * (1.0 + modulation[2:3, :]) + modulation[1:2, :]).astype(bf16)

    def row_of(wide, narrow):
        return rows.at[wide * narrows + narrow]

    def z_copy(d, of):
        return copy_to(row_of(w, n), row_of(of, n), z_sent.at[d], z_land.at[of], (g, wide_of(d), n))

    def x_copy(of, narrow):
        return copy_to(row_of(of, narrow), row_of(of, narrow), x_sent.at[of], x_land.at[of], over_x)

    def c_copy(of, narrow):
        return copy_to(
            row_of(of, narrow), row_of(of, narrow), c_sent.at[of], c_land.at[of], over_core
        )

    def d_copy(of, narrow):
        return copy_to(
            row_of(of, narrow), row_of(of, narrow), d_sent.at[of], d_land.at[of], over_core
        )

    across = (1 - x) * 2 + core
    for d in range(1, wides):
        z_copy(d, w).start()
    x_copy(w, n).start()
    c_copy(w, n).start()
    for d in range(1, wides):
        gate_copy(d, wide_of(wides - d)).wait_recv()
    experts = up.shape[0]
    which = lax.broadcasted_iota(jnp.int32, (table.shape[0], 1), 0)
    for e in range(experts):
        for of in range(wides):
            line = jnp.sum(
                jnp.where(which == w * experts + e, gates[of], 0.0), axis=0, keepdims=True
            )
            square = jnp.broadcast_to(line, (line.shape[1], line.shape[1])).T
            gate_rows[e, of * shard : (of + 1) * shard, :] = square[:shard, :]
    for d in range(1, wides):
        of = wide_of(wides - d)
        z_copy(d, of).wait_recv()
        x_copy(of, n).start()
        c_copy(of, n).start()
    def cross(d):
        of = wide_of(wides - d)
        x_copy(of, across).wait_recv()
        d_copy(of, across).start()

    def gathered(d):
        of = wide_of(wides - d)
        c_copy(of, x * 2 + 1 - core).wait_recv()
        d_copy(of, (1 - x) * 2 + 1 - core).wait_recv()

    pieces = max(1, units // 512)
    piece = units // pieces
    steps = experts * pieces

    def expand(shards, step, carry):
        e = step // pieces
        first = pl.multiple_of((step % pieces) * piece, piece)
        taken = [rows[pl.ds(of * narrows, narrows)].reshape(shard, width) for of in shards]
        made = jnp.dot(
            jnp.concatenate(taken, axis=0),
            up[e, :, pl.ds(first, piece)],
            preferred_element_type=f32,
        )
        made = jax.nn.gelu(made, approximate=True)
        columns = pl.ds(pl.multiple_of(step * piece, piece), piece)
        for k, of in enumerate(shards):
            lines = pl.ds(pl.multiple_of(of * shard, shard), shard)
            scaled = made[k * shard : (k + 1) * shard] * gate_rows[e, lines, 0:1]
            hidden[lines, columns] = scaled.astype(bf16)
        return carry

    half = wides // 2
    near = [wide_of(wides - d) for d in range(half)]
    far = [wide_of(wides - d) for d in range(half, wides)]
    for d in range(half):
        cross(d)
    load_up.wait()
    for d in range(half):
        gathered(d)
    lax.fori_loop(0, steps // 2, functools.partial(expand, near), 0)
    cross(half)
    lax.fori_loop(steps // 2, steps, functools.partial(expand, near), 0)
    for d in range(half + 1, wides):
        cross(d)
    for d in range(half, wides):
        gathered(d)
    lax.fori_loop(0, steps, functools.partial(expand, far), 0)
    load_down.wait()

    def core_copy(c):
        return copy_to(
            mixed.at[c, :, :, 1 - core], core_in.at[c], pc_sent.at[c], pc_land.at[c], over_core
        )

    def pair_copy(c):
        return copy_to(pair.at[c, :, 1 - x], x_in.at[c], px_sent.at[c], px_land.at[c], over_x)

    def quad_copy(c, d, of):
        return copy_to(
            quad.at[c, wide_of(d)],
            z_in.at[c, of],
            pz_sent.at[c * wides + d],
            pz_land.at[c * wides + of],
            (g, wide_of(d), n),
        )

    def after_core(c):
        core_copy(c).wait_recv()
        total = mixed[c, :, :, core].astype(f32) + core_in[c].astype(f32)
        pair[c] = total.astype(bf16)
        pair_copy(c).start()

    def after_x(c):
        pair_copy(c).wait_recv()
        quad[c] = (pair[c, :, x].astype(f32) + x_in[c].astype(f32)).astype(bf16)
        for d in range(1, wides):
            quad_copy(c, d, w).start()

    def after_z(c):
        total = quad[c, w].astype(f32)
        for d in range(1, wides):
            of = wide_of(wides - d)
            quad_copy(c, d, of).wait_recv()
            total = total + z_in[c, of].astype(f32)
        at = slice(c * chunk, (c + 1) * chunk)
        out[:, at] = (res[:, at] + modulation[3:4, at] * total).astype(bf16)

    for c in range(chunks):
        made = jnp.dot(
            hidden[...], down[:, c * chunk : (c + 1) * chunk], preferred_element_type=f32
        )
        mixed[c] = made.astype(bf16).reshape(wides, 2, 2, tok, chunk)
        core_copy(c).start()
        if c >= 1:
            after_core(c - 1)
    after_core(chunks - 1)
    for c in range(chunks):
        after_x(c)
    for c in range(chunks):
        after_z(c)

    def sent_qkv(d, carry):
        qkv_copy(lax.rem(me + d, everyone), me, d).wait_send()
        return carry

    lax.fori_loop(1, everyone, sent_qkv, 0)
    for d in range(1, wides):
        gate_copy(d, w).wait_send()
        att_copy(d, w).wait_send()
        z_copy(d, w).wait_send()
    for d in range(1, narrows):
        part_copy(d, n).wait_send()
    for of in range(wides):
        x_copy(of, n).wait_send()
        c_copy(of, n).wait_send()
        d_copy(of, across).wait_send()
    for c in range(chunks):
        core_copy(c).wait_send()
        pair_copy(c).wait_send()
        for d in range(1, wides):
            quad_copy(c, d, w).wait_send()


def fused(
    projected, latents, modulation, routes, route_weights, out_proj, expert_up, expert_down
):
    wides = lax.axis_size("wide")
    narrows = lax.axis_size("narrow")
    tok, width = latents.shape
    shard = tok * narrows
    seq = shard * wides
    cols = width // (wides * narrows)
    experts, unused, units = expert_up.shape
    chunks = 4
    chunk = width // chunks
    f32, bf16 = jnp.float32, jnp.bfloat16
    down = expert_down.reshape(experts * units, width)
    vmem = pl.BlockSpec(memory_space=pltpu.VMEM)
    hbm = pl.BlockSpec(memory_space=pltpu.HBM)
    dma = pltpu.SemaphoreType.DMA
    everyone = wides * narrows
    sizes = [9, everyone, everyone] + [wides] * 4 + [narrows] * 2 + [wides] * 8
    sizes += [chunks] * 4 + [chunks * wides] * 2
    return pl.pallas_call(
        functools.partial(block_kernel, wides, chunks),
        out_shape=jax.ShapeDtypeStruct((tok, width), bf16),
        in_specs=[hbm] * 8,
        out_specs=vmem,
        scratch_shapes=[
            pltpu.VMEM((2, shard), jnp.int32),
            pltpu.VMEM((2, shard), f32),
            pltpu.VMEM((experts * wides, 128), f32),
            pltpu.VMEM(projected.shape, bf16),
            pltpu.VMEM((tok, width), bf16),
            pltpu.VMEM(modulation.shape, f32),
            pltpu.VMEM(out_proj.shape, bf16),
            pltpu.VMEM(expert_up.shape, bf16),
            pltpu.VMEM(down.shape, bf16),
            pltpu.VMEM((3, everyone, tok, cols), bf16),
            pltpu.VMEM((wides, shard, cols), bf16),
            pltpu.VMEM((wides, shard, cols), bf16),
            pltpu.VMEM((narrows, tok, width), bf16),
            pltpu.VMEM((narrows, tok, width), bf16),
            pltpu.VMEM((tok, width), f32),
            pltpu.VMEM((everyone, tok, width), bf16),
            pltpu.VMEM((wides, experts * wides, 128), f32),
            pltpu.VMEM((experts, seq, 128), f32),
            pltpu.VMEM((seq, experts * units), bf16),
            pltpu.VMEM((chunks, wides, 2, 2, tok, chunk), bf16),
            pltpu.VMEM((chunks, wides, 2, tok, chunk), bf16),
            pltpu.VMEM((chunks, wides, 2, tok, chunk), bf16),
            pltpu.VMEM((chunks, wides, tok, chunk), bf16),
            pltpu.VMEM((chunks, wides, tok, chunk), bf16),
            pltpu.VMEM((chunks, wides, tok, chunk), bf16),
        ]
        + [dma((size,)) for size in sizes],
        compiler_params=pltpu.CompilerParams(
            collective_id=0, has_side_effects=True, vmem_limit_bytes=65400 * 1024
        ),
    )(projected, latents, modulation, routes.T, route_weights.T, out_proj, expert_up, down)


def solution(mesh):
    in_specs = (
        P(None, ("groups", "wide", "narrow"), None),
        P(("groups", "wide", "narrow"), None),
        P("groups", None),
        P(("groups", "wide"), None),
        P(("groups", "wide"), None),
        P("narrow", None),
        P("wide", None, "narrow"),
        P("wide", "narrow", None),
    )
    out_specs = P(("groups", "wide", "narrow"), None)
    small = mesh.shape["narrow"] == 4 and mesh.shape["wide"] == 4
    return jax.shard_map(
        fused if small else on_device,
        mesh=mesh,
        in_specs=in_specs,
        out_specs=out_specs,
        check_vma=False,
    )
```
